256 devices in a mesh: chan: 32 (over z, y_lo, core), rec: 8 (over y_hi, x).
Axes of the slice: x: 4, y: 4 (y_hi: 2, y_lo: 2; y = y_hi * 2 + y_lo), z: 8, core: 2. Of those that a mesh axis runs over, the one named last changes fastest.
Arguments:
- record: bfloat16 [8192, 64, 2000], P('chan', 'rec'), may hold values from -6 to 6
Outputs:
- stacked: float32 [64, 2, 2, 8192, 128], P('rec', None, None, 'chan')
The draws below stay inside these ranges and needn't reach their ends.
All inputs are finite; a program needn't handle non-finite values.
Results may differ from the reference program's by a relative error of at most 0.0047.
Values may be sent and summed in bfloat16 or wider, within the bound.
No kernel may reach another device: no remote copies, remote signals or barrier semaphores. Data moves between devices by JAX's collectives and lax.ppermute only.
A program may use at most 128 MiB of HBM per device.

```python
import math
import jax
import jax.numpy as jnp
from jax import lax

SAMPLES = 2000
WIDE = 512
BINS = 64
FIRST_BIN = 40
BLOCK = 128
CHANNELS = 8192
RECORDS = 64


def shard_levels(rng, dims, cuts, smallest, top_value):
    gain, own = 1.0, jax.random.fold_in(rng, 6)
    for axis_at, parts in cuts:
        heights = jnp.exp(jax.random.uniform(jax.random.fold_in(own, axis_at), (parts,), jnp.float32, smallest / len(cuts), top_value / len(cuts)))
        gain = gain * jnp.repeat(heights, dims[axis_at] // parts).reshape([-1 if axis == axis_at else 1 for axis in range(len(dims))])
    return gain


def gaussian(own_key, extent, scale, bound, pieces=(), held_as=jnp.bfloat16):
    factor_of = shard_levels(own_key, extent, pieces, -0.22, 0.18) if pieces else 1.0
    drawn = jax.random.normal(own_key, extent, jnp.float32) * scale * factor_of
    return jnp.minimum(jnp.maximum(drawn, -bound), bound).astype(held_as)


def setup_inputs(seed: int = 0) -> dict:
    key_of = jax.random.split(jax.random.key(seed), 2)
    record = gaussian(key_of[0], (CHANNELS, RECORDS, SAMPLES), 1.0, 6.0, ((0, 32), (1, 8)))
    return {"record": record}


def make_table():
    sample = jnp.arange(SAMPLES, dtype=jnp.int32)
    freq = jnp.arange(1, WIDE + 1, dtype=jnp.int32)
    phase = sample[:, None] * freq[None, :] % SAMPLES
    angle = 2.0 * math.pi / SAMPLES * phase.astype(jnp.float32)
    return jnp.concatenate([jnp.cos(angle), -jnp.sin(angle)], axis=1).astype(jnp.bfloat16)

def whiten(spectrum):
    real_part = spectrum[:, :WIDE]
    imag_part = spectrum[:, WIDE:]
    power = real_part * real_part + imag_part * imag_part
    padded = jnp.pad(power, ((0, 0), (1, 1)))
    smooth = (padded[:, :-2] + padded[:, 1:-1] + padded[:, 2:]) / 3.0
    level = lax.optimization_barrier(jnp.mean(power, axis=1, keepdims=True))
    scale = lax.rsqrt(0.5 * smooth + level + 1e-06)
    low = FIRST_BIN
    high = FIRST_BIN + BINS
    kept_scale = scale[:, low:high]
    return jnp.concatenate([real_part[:, low:high] * kept_scale, imag_part[:, low:high] * kept_scale], axis=1).astype(jnp.bfloat16)

def cross_stack(own, edge, records):
    freqs, _, recs, chans = own.shape
    width = edge.shape[3]
    before = jnp.concatenate([edge, own[..., :chans - width]], axis=3)
    mine = own.reshape(freqs, 2, recs, chans // width, width).astype(jnp.float32)
    prior = before.reshape(freqs, 2, recs, chans // width, width).astype(jnp.float32)
    left = jnp.concatenate([mine[:, 0], mine[:, 1]], axis=1)
    kinds = []
    for partner in (mine, prior):
        right_real = jnp.concatenate([partner[:, 0], partner[:, 1]], axis=1)
        right_imag = jnp.concatenate([-partner[:, 1], partner[:, 0]], axis=1)
        real_sum = jnp.einsum('frbi,frbj->fbij', left, right_real)
        imag_sum = jnp.einsum('frbi,frbj->fbij', left, right_imag)
        kinds.append(jnp.stack([real_sum, imag_sum], axis=1))
    result = jnp.stack(kinds, axis=1)
    return result.reshape(freqs, 2, 2, chans, width) / records

def reference(record):
    table = make_table()
    grouped = record.reshape(CHANNELS // BLOCK, BLOCK * RECORDS, SAMPLES)

    def one_block(rows):
        return whiten(jnp.dot(rows, table, preferred_element_type=jnp.float32))
    white = lax.map(one_block, grouped)
    spectra = white.reshape(CHANNELS, RECORDS, 2, BINS).transpose(3, 2, 1, 0)
    edge = jnp.zeros((BINS, 2, RECORDS, BLOCK), jnp.bfloat16)
    spectra_groups = spectra.reshape(BINS // 8, 8, 2, RECORDS, CHANNELS)
    edge_groups = edge.reshape(BINS // 8, 8, 2, RECORDS, BLOCK)

    def one_group(pair):
        return cross_stack(pair[0], pair[1], float(RECORDS))
    stacked = lax.map(one_group, (spectra_groups, edge_groups))
    return stacked.reshape(BINS, 2, 2, CHANNELS, BLOCK)
```

```python
import functools

import jax
import jax.numpy as jnp
import numpy as np
from jax import lax
from jax.experimental import pallas as pl
from jax.experimental.pallas import tpu as pltpu
from jax.sharding import PartitionSpec as P

SAMPLES = 2000
WIDE = 512
BINS = 64
FIRST_BIN = 40
BLOCK = 128
LOW = FIRST_BIN - 8
HIGH = FIRST_BIN + BINS + 8
NEAR = HIGH - LOW


def make_table():
    sample = np.arange(SAMPLES, dtype=np.int32)
    freq = np.arange(1, WIDE + 1, dtype=np.int32)
    phase = freq[:, None] * sample[None, :] % SAMPLES
    angle = np.float32(2.0 * np.pi / SAMPLES) * phase.astype(np.float32)
    real_part, imag_part = np.cos(angle), -np.sin(angle)
    far = np.r_[0:LOW, HIGH:WIDE]
    rows = [real_part[LOW:HIGH], imag_part[LOW:HIGH], real_part[far], imag_part[far]]
    return np.concatenate(rows, axis=0).astype(jnp.bfloat16)


def shifted(value, axis, steps):
    count = lax.axis_size(axis)
    return lax.ppermute(value, axis, [(source, source + steps) for source in range(count - steps)])


def spectra_kernel(table_ref, record_ref, out_ref, white_ref):
    step = pl.program_id(0)
    rows = record_ref[0]
    near = jnp.dot(table_ref[: 2 * NEAR], rows, preferred_element_type=jnp.float32)
    far = jnp.dot(table_ref[2 * NEAR :], rows, preferred_element_type=jnp.float32)
    real_part, imag_part = near[:NEAR], near[NEAR:]
    power = real_part * real_part + imag_part * imag_part
    total = jnp.sum(power, axis=0, keepdims=True) + jnp.sum(far * far, axis=0, keepdims=True)
    level = total * (1.0 / WIDE)
    smooth = (power[7 : 7 + BINS] + power[8 : 8 + BINS] + power[9 : 9 + BINS]) / 3.0
    scale = lax.rsqrt(0.5 * smooth + level + 1e-06)
    base = pl.multiple_of(step * 2 * BINS, 2 * BINS)
    white = [part[8 : 8 + BINS] * scale for part in (real_part, imag_part)]
    for tile in range(white_ref.shape[0]):
        lanes = slice(tile * 128, (tile + 1) * 128)
        for part in range(2):
            white_ref[tile, pl.ds(base + part * BINS, BINS), :] = white[part][:, lanes]

    @pl.when(step == pl.num_programs(0) - 1)
    def _():
        recs = out_ref.shape[1] // 2
        for index in range(BINS):
            for tile in range(white_ref.shape[0]):
                pair = [
                    white_ref[tile, pl.ds(index + part * BINS, recs, stride=2 * BINS), :]
                    for part in range(2)
                ]
                lanes = slice(tile * 128, (tile + 1) * 128)
                out_ref[index, :, lanes] = jnp.concatenate(pair, axis=0).astype(jnp.bfloat16)


def spectra(table, record):
    recs, samples, chans = record.shape
    return pl.pallas_call(
        spectra_kernel,
        grid=(recs,),
        in_specs=[
            pl.BlockSpec((2 * WIDE, samples), lambda r: (0, 0)),
            pl.BlockSpec((1, samples, chans), lambda r: (r, 0, 0)),
        ],
        out_specs=pl.BlockSpec((BINS, 2 * recs, chans), lambda r: (0, 0, 0)),
        out_shape=jax.ShapeDtypeStruct((BINS, 2 * recs, chans), jnp.bfloat16),
        scratch_shapes=[pltpu.VMEM((chans // 128, recs * 2 * BINS, 128), jnp.float32)],
        compiler_params=pltpu.CompilerParams(vmem_limit_bytes=48 * 2**20),
        cost_estimate=pl.CostEstimate(
            flops=2 * recs * samples * chans * 2 * WIDE,
            bytes_accessed=recs * samples * chans * 2,
            transcendentals=0,
        ),
        name="spectra",
    )(table, record)


def cross_kernel(scale, own_ref, edge_ref, out_ref):
    groups, _, depth, chans = own_ref.shape
    recs = depth // 2
    own = own_ref[:, 0]
    edge = edge_ref[:, 0]

    def turned(value):
        return jnp.concatenate([-value[:, recs:], value[:, :recs]], axis=1)

    def flat(value):
        return value.reshape(groups * depth, value.shape[-1])

    left = flat(own)
    right = [flat(edge), left]
    right_turned = [flat(turned(edge)), flat(turned(own))]
    for block in range(chans // BLOCK):
        here = slice(block * BLOCK, (block + 1) * BLOCK)
        if block == 0:
            prior = right[0], right_turned[0]
        else:
            before = slice((block - 1) * BLOCK, block * BLOCK)
            prior = right[1][:, before], right_turned[1][:, before]
        partners = jnp.concatenate(
            [right[1][:, here], right_turned[1][:, here], prior[0], prior[1]], axis=1
        )
        sums = lax.dot_general(
            left[:, here], partners, (((0,), (0,)), ((), ())), preferred_element_type=jnp.float32
        )
        for kind in range(2):
            for part in range(2):
                first = (2 * kind + part) * BLOCK
                out_ref[0, kind, part, here, :] = sums[:, first : first + BLOCK] * scale


def cross_stack(own, edge, records):
    groups, freqs, depth, chans = own.shape
    return pl.pallas_call(
        functools.partial(cross_kernel, 1.0 / records),
        grid=(freqs,),
        in_specs=[
            pl.BlockSpec((groups, 1, depth, chans), lambda f: (0, f, 0, 0)),
            pl.BlockSpec((groups, 1, depth, BLOCK), lambda f: (0, f, 0, 0)),
        ],
        out_specs=pl.BlockSpec((1, 2, 2, chans, BLOCK), lambda f: (f, 0, 0, 0, 0)),
        out_shape=jax.ShapeDtypeStruct((freqs, 2, 2, chans, BLOCK), jnp.float32),
        name="cross",
    )(own, edge)


def shards(record):
    chans, recs, samples = record.shape
    groups = lax.axis_size("rec")
    white = spectra(jnp.asarray(make_table()), record.transpose(1, 2, 0))
    white = white.reshape(groups, BINS // groups, 2 * recs, chans)
    own = lax.all_to_all(white, "rec", 0, 0, tiled=True)
    edge = shifted(own[..., chans - BLOCK :], "chan", 1)
    return cross_stack(own, edge, float(recs * groups))


def solution(mesh):
    in_specs = (P("chan", "rec", None),)
    out_specs = P("rec", None, None, "chan", None)
    return jax.shard_map(shards, mesh=mesh, in_specs=in_specs, out_specs=out_specs, check_vma=False)
```

```python
import functools

import jax
import jax.numpy as jnp
import numpy as np
from jax import lax
from jax.experimental import pallas as pl
from jax.experimental.pallas import tpu as pltpu
from jax.sharding import PartitionSpec as P

SAMPLES = 2000
HALF = SAMPLES // 2
WIDE = 512
BINS = 64
FIRST_BIN = 40
BLOCK = 128
NEAR = 72
AHEAD = 3
OWN_BINS = 4
EDGE_BINS = 8


def make_tables():
    sample = np.arange(SAMPLES, dtype=np.int32)
    freq = np.arange(1, WIDE + 1, dtype=np.int32)
    phase = freq[:, None] * sample[None, :] % SAMPLES
    angle = np.float32(2.0 * np.pi / SAMPLES) * phase.astype(np.float32)
    real_part, imag_part = np.cos(angle), -np.sin(angle)
    high = FIRST_BIN + BINS
    near = np.r_[FIRST_BIN:high, high, FIRST_BIN - 1, high + 1 : high + NEAR - BINS - 1]
    far = np.setdiff1d(np.arange(WIDE), near)
    even, odd = far[freq[far] % 2 == 0], far[freq[far] % 2 == 1]
    pick = lambda rows, count: np.concatenate([real_part[rows, :count], imag_part[rows, :count]])
    return [
        jnp.asarray(pick(rows, count).astype(jnp.bfloat16))
        for rows, count in ((near, SAMPLES), (even, HALF), (odd, HALF))
    ]


def shifted(value, axis, steps):
    count = lax.axis_size(axis)
    return lax.ppermute(value, axis, [(source, source + steps) for source in range(count - steps)])


def product(left, right):
    return jnp.dot(left, right, preferred_element_type=jnp.float32)


def squares(value):
    return jnp.sum((value * value).reshape(-1, 8, value.shape[-1]), axis=0)


def spectra_kernel(
    near_hbm, even_hbm, odd_hbm, record_hbm, out_ref,
    near_ref, even_ref, odd_ref, record_ref, white_ref, table_sems, record_sems,
):
    recs, _, chans = record_ref.shape

    def record_copy(rec):
        return pltpu.make_async_copy(record_hbm.at[rec], record_ref.at[rec], record_sems.at[rec])

    table_copies = [
        pltpu.make_async_copy(source, target, table_sems.at[index])
        for index, (source, target) in enumerate(
            ((near_hbm, near_ref), (even_hbm, even_ref), (odd_hbm, odd_ref))
        )
    ]
    record_copy(0).start()
    for copy in table_copies:
        copy.start()
    for rec in range(1, min(AHEAD, recs)):
        record_copy(rec).start()

    def one_record(rec, ready):
        record_copy(rec).wait()
        ready(0)
        near = product(near_ref[...], record_ref[rec])
        low, high = record_ref[rec, :HALF], record_ref[rec, HALF:]
        ready(1)
        total = squares(product(even_ref[...], low + high))
        ready(2)
        total += squares(product(odd_ref[...], low - high))
        real_part, imag_part = near[:NEAR], near[NEAR:]
        power = real_part * real_part + imag_part * imag_part
        total += jnp.sum(power.reshape(-1, 8, chans), axis=0)
        level = jnp.sum(total, axis=0, keepdims=True) * (1.0 / WIDE)
        above = power[1 : BINS + 1]
        below = jnp.concatenate([power[BINS + 1 : BINS + 2], power[: BINS - 1]], axis=0)
        scale = lax.rsqrt(0.5 * ((below + power[:BINS] + above) / 3.0) + level + 1e-06)
        white = real_part[:BINS] * scale, imag_part[:BINS] * scale
        first = rec * 2 * BINS
        if not isinstance(rec, int):
            first = pl.multiple_of(first, 2 * BINS)
        for part in range(2):
            for block in range(chans // BLOCK):
                lanes = slice(block * BLOCK, (block + 1) * BLOCK)
                white_ref[block, pl.ds(first + part * BINS, BINS), :] = white[part][:, lanes]

    def later_record(rec, _):
        @pl.when(rec + AHEAD - 1 < recs)
        def _():
            record_copy(rec + AHEAD - 1).start()

        one_record(rec, lambda index: None)
        return 0

    one_record(0, lambda index: table_copies[index].wait())
    lax.fori_loop(1, recs, later_record, 0)
    for index in range(BINS):
        for block in range(chans // BLOCK):
            both = [
                white_ref[block, pl.ds(index + part * BINS, recs, stride=2 * BINS), :]
                for part in range(2)
            ]
            lanes = slice(block * BLOCK, (block + 1) * BLOCK)
            out_ref[index, :, lanes] = jnp.concatenate(both, axis=0).astype(jnp.bfloat16)


def spectra(tables, record):
    recs, samples, chans = record.shape
    rows = sum(table.shape[0] * table.shape[1] for table in tables)
    return pl.pallas_call(
        spectra_kernel,
        in_specs=[pl.BlockSpec(memory_space=pltpu.HBM)] * 4,
        out_specs=pl.BlockSpec(memory_space=pltpu.VMEM),
        out_shape=jax.ShapeDtypeStruct((BINS, 2 * recs, chans), jnp.bfloat16),
        scratch_shapes=[pltpu.VMEM(table.shape, table.dtype) for table in tables]
        + [
            pltpu.VMEM(record.shape, jnp.bfloat16),
            pltpu.VMEM((chans // BLOCK, recs * 2 * BINS, BLOCK), jnp.float32),
            pltpu.SemaphoreType.DMA((3,)),
            pltpu.SemaphoreType.DMA((recs,)),
        ],
        compiler_params=pltpu.CompilerParams(vmem_limit_bytes=60 * 2**20),
        cost_estimate=pl.CostEstimate(
            flops=2 * recs * chans * rows,
            bytes_accessed=2 * (recs * samples * chans + rows),
            transcendentals=recs * chans * BINS,
        ),
        name="spectra",
    )(*tables, record)


def turned(value):
    recs = value.shape[1] // 2
    wide = value.astype(jnp.float32)
    other = jnp.concatenate([wide[:, recs:], -wide[:, :recs]], axis=1)
    return other.astype(jnp.bfloat16)


def flat(value):
    return value.reshape(-1, value.shape[-1])


def against(left, right):
    return lax.dot_general(left, right, (((0,), (0,)), ((), ())), preferred_element_type=jnp.float32)


def own_kernel(scale, own_ref, out_ref):
    bins = out_ref.shape[0]
    for bin_at in range(bins):
        own = own_ref[:, pl.program_id(0) * bins + bin_at]
        both = flat(own), flat(turned(own))
        for block in range(own.shape[-1] // BLOCK):
            here = slice(block * BLOCK, (block + 1) * BLOCK)
            first = max(block - 1, 0) * BLOCK
            for part in range(2):
                sums = against(both[part][:, here], both[0][:, first : (block + 1) * BLOCK]) * scale
                out_ref[bin_at, 0, part, here, :] = sums[:, -BLOCK:]
                if block:
                    out_ref[bin_at, 1, part, here, :] = sums[:, :BLOCK]


def edge_kernel(scale, own_ref, edge_ref, _, out_ref):
    bins = out_ref.shape[0]
    for bin_at in range(bins):
        row = pl.program_id(0) * bins + bin_at
        own = own_ref[:, row, :, :BLOCK]
        edge = flat(edge_ref[:, row])
        both = flat(own), flat(turned(own))
        for part in range(2):
            out_ref[bin_at, 0, part] = against(both[part], edge) * scale


def own_stack(own, records):
    groups, freqs, depth, chans = own.shape
    return pl.pallas_call(
        functools.partial(own_kernel, 1.0 / records),
        grid=(freqs // OWN_BINS,),
        in_specs=[pl.BlockSpec(memory_space=pltpu.VMEM)],
        out_specs=pl.BlockSpec((OWN_BINS, 2, 2, chans, BLOCK), lambda f: (f, 0, 0, 0, 0)),
        out_shape=jax.ShapeDtypeStruct((freqs, 2, 2, chans, BLOCK), jnp.float32),
        compiler_params=pltpu.CompilerParams(vmem_limit_bytes=16 * 2**20),
        cost_estimate=pl.CostEstimate(
            flops=2 * freqs * chans * groups * depth * 3 * BLOCK,
            bytes_accessed=freqs * 4 * chans * BLOCK * 4,
            transcendentals=0,
        ),
        name="own",
    )(own)


def edge_stack(own, edge, stack, records):
    groups, freqs, depth, chans = own.shape
    return pl.pallas_call(
        functools.partial(edge_kernel, 1.0 / records),
        grid=(freqs // EDGE_BINS,),
        in_specs=[pl.BlockSpec(memory_space=pltpu.VMEM)] * 2 + [pl.BlockSpec(memory_space=pl.ANY)],
        out_specs=pl.BlockSpec((EDGE_BINS, 1, 2, BLOCK, BLOCK), lambda f: (f, 1, 0, 0, 0)),
        out_shape=jax.ShapeDtypeStruct(stack.shape, stack.dtype),
        input_output_aliases={2: 0},
        compiler_params=pltpu.CompilerParams(vmem_limit_bytes=16 * 2**20),
        cost_estimate=pl.CostEstimate(
            flops=2 * freqs * BLOCK * groups * depth * 2 * BLOCK,
            bytes_accessed=freqs * 2 * BLOCK * BLOCK * 4,
            transcendentals=0,
        ),
        name="edge",
    )(own, edge, stack)


def shards(record):
    chans, recs, _ = record.shape
    groups = lax.axis_size("rec")
    records = float(recs * groups)
    white = spectra(make_tables(), record.transpose(1, 2, 0))
    white = white.reshape(groups, BINS // groups, 2 * recs, chans)
    own = lax.all_to_all(white, "rec", 0, 0, tiled=True)
    edge = shifted(own[..., chans - BLOCK :], "chan", 1)
    return edge_stack(own, edge, own_stack(own, records), records)


def solution(mesh):
    in_specs = (P("chan", "rec", None),)
    out_specs = P("rec", None, None, "chan", None)
    return jax.shard_map(shards, mesh=mesh, in_specs=in_specs, out_specs=out_specs, check_vma=False)
```

```python
import functools

import jax
import jax.numpy as jnp
import numpy as np
from jax import lax
from jax.experimental import pallas as pl
from jax.experimental.pallas import tpu as pltpu
from jax.sharding import PartitionSpec as P

SAMPLES = 2000
HALF = SAMPLES // 2
QUARTER = SAMPLES // 4
WIDE = 512
BINS = 64
FIRST_BIN = 40
BLOCK = 128
NEAR = 72
AHEAD = 3
OWN_BINS = 4
EDGE_BINS = 8


def make_tables():
    sample = np.arange(SAMPLES, dtype=np.int32)
    freq = np.arange(1, WIDE + 1, dtype=np.int32)
    phase = freq[:, None] * sample[None, :] % SAMPLES
    angle = np.float32(2.0 * np.pi / SAMPLES) * phase.astype(np.float32)
    real_part, imag_part = np.cos(angle), -np.sin(angle)
    high = FIRST_BIN + BINS
    near = np.r_[FIRST_BIN:high, high, FIRST_BIN - 1, high + 1 : high + NEAR - BINS - 1]
    far = np.setdiff1d(np.arange(WIDE), near)
    rest = freq[far] % 4
    parts = (
        (near, SAMPLES),
        (far[rest == 0], QUARTER),
        (far[rest == 2], QUARTER),
        (far[rest % 2 == 1], HALF),
    )
    tables = []
    for bins, count in parts:
        rows = np.concatenate([real_part[bins, :count], imag_part[bins, :count]])
        rows = np.pad(rows, ((0, -len(rows) % 16), (0, 0)))
        tables.append(jnp.asarray(rows.astype(jnp.bfloat16)))
    return tables


def turned_on(value, axis):
    count = lax.axis_size(axis)
    return lax.ppermute(value, axis, [(source, (source + 1) % count) for source in range(count)])


def product(left, right):
    return jnp.dot(left, right, preferred_element_type=jnp.float32)


def squares(value):
    return jnp.sum((value * value).reshape(-1, 8, value.shape[-1]), axis=0)


def spectra_kernel(
    near_hbm, fours_hbm, twos_hbm, odds_hbm, record_hbm, out_ref,
    near_ref, fours_ref, twos_ref, odds_ref, record_ref, white_ref, table_sems, record_sems,
):
    recs, _, chans = record_ref.shape
    tables_hbm = near_hbm, fours_hbm, twos_hbm, odds_hbm
    tables = near_ref, fours_ref, twos_ref, odds_ref

    def record_copy(rec):
        return pltpu.make_async_copy(record_hbm.at[rec], record_ref.at[rec], record_sems.at[rec])

    table_copies = [
        pltpu.make_async_copy(source, target, table_sems.at[index])
        for index, (source, target) in enumerate(zip(tables_hbm, tables))
    ]
    record_copy(0).start()
    for copy in table_copies:
        copy.start()
    for rec in range(1, min(AHEAD, recs)):
        record_copy(rec).start()

    def one_record(rec, ready):
        record_copy(rec).wait()
        ready(0)
        near = product(near_ref[...], record_ref[rec])
        low, high = record_ref[rec, :HALF], record_ref[rec, HALF:]
        both = low + high
        low_both, high_both = both[:QUARTER], both[QUARTER:]
        ready(1)
        total = squares(product(fours_ref[...], low_both + high_both))
        ready(2)
        total += squares(product(twos_ref[...], low_both - high_both))
        ready(3)
        total += squares(product(odds_ref[...], low - high))
        real_part, imag_part = near[:NEAR], near[NEAR:]
        power = real_part * real_part + imag_part * imag_part
        total += jnp.sum(power.reshape(-1, 8, chans), axis=0)
        level = jnp.sum(total, axis=0, keepdims=True) * (1.0 / WIDE)
        above = power[1 : BINS + 1]
        below = jnp.concatenate([power[BINS + 1 : BINS + 2], power[: BINS - 1]], axis=0)
        scale = lax.rsqrt(0.5 * ((below + power[:BINS] + above) / 3.0) + level + 1e-06)
        white = real_part[:BINS] * scale, imag_part[:BINS] * scale
        first = rec * 2 * BINS
        if not isinstance(rec, int):
            first = pl.multiple_of(first, 2 * BINS)
        for part in range(2):
            for block in range(chans // BLOCK):
                lanes = slice(block * BLOCK, (block + 1) * BLOCK)
                white_ref[block, pl.ds(first + part * BINS, BINS), :] = white[part][:, lanes]

    def later_record(rec, _):
        @pl.when(rec + AHEAD - 1 < recs)
        def _():
            record_copy(rec + AHEAD - 1).start()

        one_record(rec, lambda index: None)
        return 0

    one_record(0, lambda index: table_copies[index].wait())
    lax.fori_loop(1, recs, later_record, 0)
    for index in range(BINS):
        for block in range(chans // BLOCK):
            both = [
                white_ref[block, pl.ds(index + part * BINS, recs, stride=2 * BINS), :]
                for part in range(2)
            ]
            lanes = slice(block * BLOCK, (block + 1) * BLOCK)
            out_ref[index, :, lanes] = jnp.concatenate(both, axis=0).astype(jnp.bfloat16)


def spectra(tables, record):
    recs, samples, chans = record.shape
    rows = sum(table.shape[0] * table.shape[1] for table in tables)
    return pl.pallas_call(
        spectra_kernel,
        in_specs=[pl.BlockSpec(memory_space=pltpu.HBM)] * (len(tables) + 1),
        out_specs=pl.BlockSpec(memory_space=pltpu.VMEM),
        out_shape=jax.ShapeDtypeStruct((BINS, 2 * recs, chans), jnp.bfloat16),
        scratch_shapes=[pltpu.VMEM(table.shape, table.dtype) for table in tables]
        + [
            pltpu.VMEM(record.shape, jnp.bfloat16),
            pltpu.VMEM((chans // BLOCK, recs * 2 * BINS, BLOCK), jnp.float32),
            pltpu.SemaphoreType.DMA((len(tables),)),
            pltpu.SemaphoreType.DMA((recs,)),
        ],
        compiler_params=pltpu.CompilerParams(vmem_limit_bytes=60 * 2**20),
        cost_estimate=pl.CostEstimate(
            flops=2 * recs * chans * rows,
            bytes_accessed=2 * (recs * samples * chans + rows),
            transcendentals=recs * chans * BINS,
        ),
        name="spectra",
    )(*tables, record)


def turned(value):
    recs = value.shape[1] // 2
    wide = value.astype(jnp.float32)
    other = jnp.concatenate([wide[:, recs:], -wide[:, :recs]], axis=1)
    return other.astype(jnp.bfloat16)


def flat(value):
    return value.reshape(-1, value.shape[-1])


def against(left, right):
    return lax.dot_general(left, right, (((0,), (0,)), ((), ())), preferred_element_type=jnp.float32)


def own_kernel(scale, own_ref, out_ref):
    bins = out_ref.shape[0]
    for bin_at in range(bins):
        own = own_ref[:, pl.program_id(0) * bins + bin_at]
        both = flat(own), flat(turned(own))
        for block in range(own.shape[-1] // BLOCK):
            here = slice(block * BLOCK, (block + 1) * BLOCK)
            first = max(block - 1, 0) * BLOCK
            for part in range(2):
                sums = against(both[part][:, here], both[0][:, first : (block + 1) * BLOCK]) * scale
                out_ref[bin_at, 0, part, here, :] = sums[:, -BLOCK:]
                if block:
                    out_ref[bin_at, 1, part, here, :] = sums[:, :BLOCK]


def edge_kernel(scale, place_ref, own_ref, edge_ref, _, out_ref):
    bins = out_ref.shape[0]
    inside = place_ref[0] > 0
    for bin_at in range(bins):
        row = pl.program_id(0) * bins + bin_at
        own = own_ref[:, row, :, :BLOCK]
        edge = flat(edge_ref[:, row])
        both = flat(own), flat(turned(own))
        for part in range(2):
            out_ref[bin_at, 0, part] = jnp.where(inside, against(both[part], edge) * scale, 0.0)


def own_stack(own, records):
    groups, freqs, depth, chans = own.shape
    return pl.pallas_call(
        functools.partial(own_kernel, 1.0 / records),
        grid=(freqs // OWN_BINS,),
        in_specs=[pl.BlockSpec(memory_space=pltpu.VMEM)],
        out_specs=pl.BlockSpec((OWN_BINS, 2, 2, chans, BLOCK), lambda f: (f, 0, 0, 0, 0)),
        out_shape=jax.ShapeDtypeStruct((freqs, 2, 2, chans, BLOCK), jnp.float32),
        compiler_params=pltpu.CompilerParams(vmem_limit_bytes=16 * 2**20),
        cost_estimate=pl.CostEstimate(
            flops=2 * freqs * chans * groups * depth * 3 * BLOCK,
            bytes_accessed=freqs * 4 * chans * BLOCK * 4,
            transcendentals=0,
        ),
        name="own",
    )(own)


def edge_stack(place, own, edge, stack, records):
    groups, freqs, depth, chans = own.shape
    return pl.pallas_call(
        functools.partial(edge_kernel, 1.0 / records),
        grid=(freqs // EDGE_BINS,),
        in_specs=[
            pl.BlockSpec(memory_space=pltpu.SMEM),
            pl.BlockSpec(memory_space=pltpu.VMEM),
            pl.BlockSpec(memory_space=pltpu.VMEM),
            pl.BlockSpec(memory_space=pl.ANY),
        ],
        out_specs=pl.BlockSpec((EDGE_BINS, 1, 2, BLOCK, BLOCK), lambda f: (f, 1, 0, 0, 0)),
        out_shape=jax.ShapeDtypeStruct(stack.shape, stack.dtype),
        input_output_aliases={3: 0},
        compiler_params=pltpu.CompilerParams(vmem_limit_bytes=16 * 2**20),
        cost_estimate=pl.CostEstimate(
            flops=2 * freqs * BLOCK * groups * depth * 2 * BLOCK,
            bytes_accessed=freqs * 2 * BLOCK * BLOCK * 4,
            transcendentals=0,
        ),
        name="edge",
    )(place, own, edge, stack)


def shards(record):
    chans, recs, _ = record.shape
    groups = lax.axis_size("rec")
    records = float(recs * groups)
    white = spectra(make_tables(), record.transpose(1, 2, 0))
    white = white.reshape(groups, BINS // groups, 2 * recs, chans)
    own = lax.all_to_all(white, "rec", 0, 0, tiled=True)
    edge = turned_on(own[..., chans - BLOCK :], "chan")
    place = lax.axis_index("chan").reshape(1)
    return edge_stack(place, own, edge, own_stack(own, records), records)


def solution(mesh):
    in_specs = (P("chan", "rec", None),)
    out_specs = P("rec", None, None, "chan", None)
    return jax.shard_map(shards, mesh=mesh, in_specs=in_specs, out_specs=out_specs, check_vma=False)
```

```python
import functools

import jax
import jax.numpy as jnp
import numpy as np
from jax import lax
from jax.experimental import pallas as pl
from jax.experimental.pallas import tpu as pltpu
from jax.sharding import PartitionSpec as P

SAMPLES = 2000
HALF = SAMPLES // 2
QUARTER = SAMPLES // 4
WIDE = 512
BINS = 64
FIRST_BIN = 40
BLOCK = 128
NEAR = 72
AHEAD = 3
OWN_BINS = 4
EDGE_BINS = 8


def make_tables():
    sample = np.arange(SAMPLES, dtype=np.int32)
    freq = np.arange(1, WIDE + 1, dtype=np.int32)
    phase = freq[:, None] * sample[None, :] % SAMPLES
    angle = np.float32(2.0 * np.pi / SAMPLES) * phase.astype(np.float32)
    real_part, imag_part = np.cos(angle), -np.sin(angle)
    high = FIRST_BIN + BINS
    near = np.r_[FIRST_BIN:high, high, FIRST_BIN - 1, high + 1 : high + NEAR - BINS - 1]
    far = np.setdiff1d(np.arange(WIDE), near)
    rest = freq[far] % 4
    parts = (
        (near, SAMPLES),
        (far[rest == 0], QUARTER),
        (far[rest == 2], QUARTER),
        (far[rest % 2 == 1], HALF),
    )
    tables = []
    for bins, count in parts:
        rows = np.concatenate([real_part[bins, :count], imag_part[bins, :count]])
        rows = np.pad(rows, ((0, -len(rows) % 16), (0, 0)))
        tables.append(jnp.asarray(rows.astype(jnp.bfloat16)))
    return tables


def turned_on(value, axis):
    count = lax.axis_size(axis)
    return lax.ppermute(value, axis, [(source, (source + 1) % count) for source in range(count)])


def product(left, right):
    return jnp.dot(left, right, preferred_element_type=jnp.float32)


def squares(value):
    return jnp.sum((value * value).reshape(-1, 8, value.shape[-1]), axis=0)


def spectra_kernel(
    near_hbm, fours_hbm, twos_hbm, odds_hbm, record_hbm, out_ref,
    near_ref, fours_ref, twos_ref, odds_ref, record_ref, found_ref, total_ref, white_ref, table_sems,
    record_sems,
):
    recs, _, chans = record_ref.shape
    tables_hbm = near_hbm, fours_hbm, twos_hbm, odds_hbm
    tables = near_ref, fours_ref, twos_ref, odds_ref

    def record_copy(rec):
        return pltpu.make_async_copy(record_hbm.at[rec], record_ref.at[rec], record_sems.at[rec])

    table_copies = [
        pltpu.make_async_copy(source, target, table_sems.at[index])
        for index, (source, target) in enumerate(zip(tables_hbm, tables))
    ]
    record_copy(0).start()
    for copy in table_copies:
        copy.start()
    record_copy(1).start()

    def whiten(rec):
        near = found_ref[rec % 2]
        total = total_ref[rec % 2]
        real_part, imag_part = near[:NEAR], near[NEAR:]
        power = real_part * real_part + imag_part * imag_part
        total += jnp.sum(power.reshape(-1, 8, chans), axis=0)
        level = jnp.sum(total, axis=0, keepdims=True) * (1.0 / WIDE)
        above = power[1 : BINS + 1]
        below = jnp.concatenate([power[BINS + 1 : BINS + 2], power[: BINS - 1]], axis=0)
        scale = lax.rsqrt(0.5 * ((below + power[:BINS] + above) / 3.0) + level + 1e-06)
        white = real_part[:BINS] * scale, imag_part[:BINS] * scale
        first = rec * 2 * BINS
        if not isinstance(rec, int):
            first = pl.multiple_of(first, 2 * BINS)
        for part in range(2):
            for block in range(chans // BLOCK):
                lanes = slice(block * BLOCK, (block + 1) * BLOCK)
                white_ref[block, pl.ds(first + part * BINS, BINS), :] = white[part][:, lanes]

    def one_record(rec, _):
        @pl.when((rec > 0) & (rec + AHEAD - 1 < recs))
        def _():
            record_copy(rec + AHEAD - 1).start()

        record_copy(rec).wait()
        whiten(jnp.maximum(rec - 1, 0))
        found = product(near_ref[...], record_ref[rec])
        low, high = record_ref[rec, :HALF], record_ref[rec, HALF:]
        both = low + high
        low_both, high_both = both[:QUARTER], both[QUARTER:]
        total = squares(product(fours_ref[...], low_both + high_both))
        total += squares(product(twos_ref[...], low_both - high_both))
        total += squares(product(odds_ref[...], low - high))
        found_ref[rec % 2] = found
        total_ref[rec % 2] = total
        return 0

    for copy in table_copies:
        copy.wait()
    for rec in range(2, min(AHEAD, recs)):
        record_copy(rec).start()
    lax.fori_loop(0, recs, one_record, 0)
    whiten(recs - 1)
    for index in range(BINS):
        for block in range(chans // BLOCK):
            both = [
                white_ref[block, pl.ds(index + part * BINS, recs, stride=2 * BINS), :]
                for part in range(2)
            ]
            lanes = slice(block * BLOCK, (block + 1) * BLOCK)
            out_ref[index, :, lanes] = jnp.concatenate(both, axis=0).astype(jnp.bfloat16)


def spectra(tables, record):
    recs, samples, chans = record.shape
    rows = sum(table.shape[0] * table.shape[1] for table in tables)
    return pl.pallas_call(
        spectra_kernel,
        in_specs=[pl.BlockSpec(memory_space=pltpu.HBM)] * (len(tables) + 1),
        out_specs=pl.BlockSpec(memory_space=pltpu.VMEM),
        out_shape=jax.ShapeDtypeStruct((BINS, 2 * recs, chans), jnp.bfloat16),
        scratch_shapes=[pltpu.VMEM(table.shape, table.dtype) for table in tables]
        + [
            pltpu.VMEM(record.shape, jnp.bfloat16),
            pltpu.VMEM((2, 2 * NEAR, chans), jnp.float32),
            pltpu.VMEM((2, 8, chans), jnp.float32),
            pltpu.VMEM((chans // BLOCK, recs * 2 * BINS, BLOCK), jnp.float32),
            pltpu.SemaphoreType.DMA((len(tables),)),
            pltpu.SemaphoreType.DMA((recs,)),
        ],
        compiler_params=pltpu.CompilerParams(vmem_limit_bytes=60 * 2**20),
        cost_estimate=pl.CostEstimate(
            flops=2 * recs * chans * rows,
            bytes_accessed=2 * (recs * samples * chans + rows),
            transcendentals=recs * chans * BINS,
        ),
        name="spectra",
    )(*tables, record)


def turned(value):
    recs = value.shape[1] // 2
    wide = value.astype(jnp.float32)
    other = jnp.concatenate([wide[:, recs:], -wide[:, :recs]], axis=1)
    return other.astype(jnp.bfloat16)


def flat(value):
    return value.reshape(-1, value.shape[-1])


def against(left, right):
    return lax.dot_general(left, right, (((0,), (0,)), ((), ())), preferred_element_type=jnp.float32)


def own_kernel(scale, own_ref, out_ref):
    bins = out_ref.shape[0]
    for bin_at in range(bins):
        own = own_ref[:, pl.program_id(0) * bins + bin_at]
        both = flat(own), flat(turned(own))
        for block in range(own.shape[-1] // BLOCK):
            here = slice(block * BLOCK, (block + 1) * BLOCK)
            first = max(block - 1, 0) * BLOCK
            for part in range(2):
                sums = against(both[part][:, here], both[0][:, first : (block + 1) * BLOCK]) * scale
                out_ref[bin_at, 0, part, here, :] = sums[:, -BLOCK:]
                if block:
                    out_ref[bin_at, 1, part, here, :] = sums[:, :BLOCK]


def edge_kernel(scale, place_ref, own_ref, edge_ref, _, out_ref):
    bins = out_ref.shape[0]
    inside = place_ref[0] > 0
    for bin_at in range(bins):
        row = pl.program_id(0) * bins + bin_at
        own = own_ref[:, row, :, :BLOCK]
        edge = flat(edge_ref[:, row])
        both = flat(own), flat(turned(own))
        for part in range(2):
            out_ref[bin_at, 0, part] = jnp.where(inside, against(both[part], edge) * scale, 0.0)


def own_stack(own, records):
    groups, freqs, depth, chans = own.shape
    return pl.pallas_call(
        functools.partial(own_kernel, 1.0 / records),
        grid=(freqs // OWN_BINS,),
        in_specs=[pl.BlockSpec(memory_space=pltpu.VMEM)],
        out_specs=pl.BlockSpec((OWN_BINS, 2, 2, chans, BLOCK), lambda f: (f, 0, 0, 0, 0)),
        out_shape=jax.ShapeDtypeStruct((freqs, 2, 2, chans, BLOCK), jnp.float32),
        compiler_params=pltpu.CompilerParams(vmem_limit_bytes=16 * 2**20),
        cost_estimate=pl.CostEstimate(
            flops=2 * freqs * chans * groups * depth * 3 * BLOCK,
            bytes_accessed=freqs * 4 * chans * BLOCK * 4,
            transcendentals=0,
        ),
        name="own",
    )(own)


def edge_stack(place, own, edge, stack, records):
    groups, freqs, depth, chans = own.shape
    return pl.pallas_call(
        functools.partial(edge_kernel, 1.0 / records),
        grid=(freqs // EDGE_BINS,),
        in_specs=[
            pl.BlockSpec(memory_space=pltpu.SMEM),
            pl.BlockSpec(memory_space=pltpu.VMEM),
            pl.BlockSpec(memory_space=pltpu.VMEM),
            pl.BlockSpec(memory_space=pl.ANY),
        ],
        out_specs=pl.BlockSpec((EDGE_BINS, 1, 2, BLOCK, BLOCK), lambda f: (f, 1, 0, 0, 0)),
        out_shape=jax.ShapeDtypeStruct(stack.shape, stack.dtype),
        input_output_aliases={3: 0},
        compiler_params=pltpu.CompilerParams(vmem_limit_bytes=16 * 2**20),
        cost_estimate=pl.CostEstimate(
            flops=2 * freqs * BLOCK * groups * depth * 2 * BLOCK,
            bytes_accessed=freqs * 2 * BLOCK * BLOCK * 4,
            transcendentals=0,
        ),
        name="edge",
    )(place, own, edge, stack)


def shards(record):
    chans, recs, _ = record.shape
    groups = lax.axis_size("rec")
    records = float(recs * groups)
    white = spectra(make_tables(), record.transpose(1, 2, 0))
    white = white.reshape(groups, BINS // groups, 2 * recs, chans)
    own = lax.all_to_all(white, "rec", 0, 0, tiled=True)
    edge = turned_on(own[..., chans - BLOCK :], "chan")
    place = lax.axis_index("chan").reshape(1)
    return edge_stack(place, own, edge, own_stack(own, records), records)


def solution(mesh):
    in_specs = (P("chan", "rec", None),)
    out_specs = P("rec", None, None, "chan", None)
    return jax.shard_map(shards, mesh=mesh, in_specs=in_specs, out_specs=out_specs, check_vma=False)
```

```python
import functools

import jax
import jax.numpy as jnp
import numpy as np
from jax import lax
from jax.experimental import pallas as pl
from jax.experimental.pallas import tpu as pltpu
from jax.sharding import PartitionSpec as P

SAMPLES = 2000
HALF = SAMPLES // 2
QUARTER = SAMPLES // 4
WIDE = 512
BINS = 64
FIRST_BIN = 40
BLOCK = 128
NEAR = 72
AHEAD = 3
OWN_BINS = 4
EDGE_BINS = 4


def make_tables():
    sample = np.arange(SAMPLES, dtype=np.int32)
    freq = np.arange(1, WIDE + 1, dtype=np.int32)
    phase = freq[:, None] * sample[None, :] % SAMPLES
    angle = np.float32(2.0 * np.pi / SAMPLES) * phase.astype(np.float32)
    real_part, imag_part = np.cos(angle), -np.sin(angle)
    high = FIRST_BIN + BINS
    near = np.r_[FIRST_BIN:high, high, FIRST_BIN - 1, high + 1 : high + NEAR - BINS - 1]
    far = np.setdiff1d(np.arange(WIDE), near)
    rest = freq[far] % 4
    parts = (
        (near, SAMPLES),
        (far[rest == 0], QUARTER),
        (far[rest == 2], QUARTER),
        (far[rest % 2 == 1], HALF),
    )
    tables = []
    for bins, count in parts:
        rows = np.concatenate([real_part[bins, :count], imag_part[bins, :count]])
        rows = np.pad(rows, ((0, -len(rows) % 16), (0, 0)))
        tables.append(jnp.asarray(rows.astype(jnp.bfloat16)))
    return tables


def turned_on(value, axis):
    count = lax.axis_size(axis)
    return lax.ppermute(value, axis, [(source, (source + 1) % count) for source in range(count)])


def product(left, right):
    return jnp.dot(left, right, preferred_element_type=jnp.float32)


def squares(value):
    return jnp.sum((value * value).reshape(-1, 8, value.shape[-1]), axis=0)


def spectra_kernel(
    near_hbm, fours_hbm, twos_hbm, odds_hbm, record_hbm, out_ref,
    near_ref, fours_ref, twos_ref, odds_ref, record_ref, found_ref, total_ref, white_ref, table_sems,
    record_sems,
):
    recs, _, chans = record_ref.shape
    tables_hbm = near_hbm, fours_hbm, twos_hbm, odds_hbm
    tables = near_ref, fours_ref, twos_ref, odds_ref

    def record_copy(rec):
        return pltpu.make_async_copy(record_hbm.at[rec], record_ref.at[rec], record_sems.at[rec])

    table_copies = [
        pltpu.make_async_copy(source, target, table_sems.at[index])
        for index, (source, target) in enumerate(zip(tables_hbm, tables))
    ]
    record_copy(0).start()
    for copy in table_copies:
        copy.start()
    record_copy(1).start()

    def whiten(rec):
        near = found_ref[rec % 2]
        total = total_ref[rec % 2]
        real_part, imag_part = near[:NEAR], near[NEAR:]
        power = real_part * real_part + imag_part * imag_part
        total += jnp.sum(power.reshape(-1, 8, chans), axis=0)
        level = jnp.sum(total, axis=0, keepdims=True) * (1.0 / WIDE)
        above = power[1 : BINS + 1]
        below = jnp.concatenate([power[BINS + 1 : BINS + 2], power[: BINS - 1]], axis=0)
        scale = lax.rsqrt(0.5 * ((below + power[:BINS] + above) / 3.0) + level + 1e-06)
        white = real_part[:BINS] * scale, imag_part[:BINS] * scale
        first = rec * 2 * BINS
        if not isinstance(rec, int):
            first = pl.multiple_of(first, 2 * BINS)
        for part in range(2):
            for block in range(chans // BLOCK):
                lanes = slice(block * BLOCK, (block + 1) * BLOCK)
                white_ref[block, pl.ds(first + part * BINS, BINS), :] = white[part][:, lanes]

    def one_record(rec, _):
        @pl.when((rec > 0) & (rec + AHEAD - 1 < recs))
        def _():
            record_copy(rec + AHEAD - 1).start()

        record_copy(rec).wait()
        whiten(jnp.maximum(rec - 1, 0))
        found = product(near_ref[...], record_ref[rec])
        low, high = record_ref[rec, :HALF], record_ref[rec, HALF:]
        both = low + high
        low_both, high_both = both[:QUARTER], both[QUARTER:]
        total = squares(product(fours_ref[...], low_both + high_both))
        total += squares(product(twos_ref[...], low_both - high_both))
        total += squares(product(odds_ref[...], low - high))
        found_ref[rec % 2] = found
        total_ref[rec % 2] = total
        return 0

    for copy in table_copies:
        copy.wait()
    for rec in range(2, min(AHEAD, recs)):
        record_copy(rec).start()
    lax.fori_loop(0, recs, one_record, 0)
    whiten(recs - 1)
    for index in range(BINS):
        for block in range(chans // BLOCK):
            both = [
                white_ref[block, pl.ds(index + part * BINS, recs, stride=2 * BINS), :]
                for part in range(2)
            ]
            lanes = slice(block * BLOCK, (block + 1) * BLOCK)
            out_ref[index, :, lanes] = jnp.concatenate(both, axis=0).astype(jnp.bfloat16)


def spectra(tables, record):
    recs, samples, chans = record.shape
    rows = sum(table.shape[0] * table.shape[1] for table in tables)
    return pl.pallas_call(
        spectra_kernel,
        in_specs=[pl.BlockSpec(memory_space=pltpu.HBM)] * (len(tables) + 1),
        out_specs=pl.BlockSpec(memory_space=pltpu.VMEM),
        out_shape=jax.ShapeDtypeStruct((BINS, 2 * recs, chans), jnp.bfloat16),
        scratch_shapes=[pltpu.VMEM(table.shape, table.dtype) for table in tables]
        + [
            pltpu.VMEM(record.shape, jnp.bfloat16),
            pltpu.VMEM((2, 2 * NEAR, chans), jnp.float32),
            pltpu.VMEM((2, 8, chans), jnp.float32),
            pltpu.VMEM((chans // BLOCK, (recs + 1) * 2 * BINS, BLOCK), jnp.float32),
            pltpu.SemaphoreType.DMA((len(tables),)),
            pltpu.SemaphoreType.DMA((recs,)),
        ],
        compiler_params=pltpu.CompilerParams(vmem_limit_bytes=60 * 2**20),
        cost_estimate=pl.CostEstimate(
            flops=2 * recs * chans * rows,
            bytes_accessed=2 * (recs * samples * chans + rows),
            transcendentals=recs * chans * BINS,
        ),
        name="spectra",
    )(*tables, record)


def turned(value):
    recs = value.shape[1] // 2
    wide = value.astype(jnp.float32)
    other = jnp.concatenate([wide[:, recs:], -wide[:, :recs]], axis=1)
    return other.astype(jnp.bfloat16)


def flat(value):
    return value.reshape(-1, value.shape[-1])


def against(left, right):
    return lax.dot_general(left, right, (((0,), (0,)), ((), ())), preferred_element_type=jnp.float32)


def own_kernel(scale, place_ref, own_ref, out_ref, left_ref):
    bins = out_ref.shape[0]
    inside = place_ref[0] > 0
    for bin_at in range(bins):
        own = own_ref[:, pl.program_id(0) * bins + bin_at]
        row = pl.program_id(0) * bins + bin_at
        both = flat(own), flat(turned(own))
        for block in range(own.shape[-1] // BLOCK):
            here = slice(block * BLOCK, (block + 1) * BLOCK)
            first = max(block - 1, 0) * BLOCK
            for part in range(2):
                left = both[part][:, here].T
                if block == 0:
                    left_ref[row, part] = jnp.where(inside, left, jnp.zeros_like(left))
                sums = product(left, both[0][:, first : (block + 1) * BLOCK]) * scale
                out_ref[bin_at, 0, part, here, :] = sums[:, -BLOCK:]
                if block:
                    out_ref[bin_at, 1, part, here, :] = sums[:, :BLOCK]


def edge_kernel(scale, first_bin, left_ref, edge_ref, _, out_ref, sums_ref, sems):
    bins = edge_ref.shape[1]
    copies = []
    for bin_at in range(bins):
        edge = flat(edge_ref[:, bin_at])
        for part in range(2):
            sums_ref[bin_at, part] = product(left_ref[first_bin + bin_at, part], edge) * scale
        copies.append(
            pltpu.make_async_copy(
                sums_ref.at[bin_at],
                out_ref.at[first_bin + bin_at, 1, :, pl.ds(0, BLOCK), :],
                sems.at[bin_at],
            )
        )
        copies[-1].start()
    for copy in copies:
        copy.wait()


def own_stack(place, own, records):
    groups, freqs, depth, chans = own.shape
    return pl.pallas_call(
        functools.partial(own_kernel, 1.0 / records),
        grid=(freqs // OWN_BINS,),
        in_specs=[pl.BlockSpec(memory_space=pltpu.SMEM), pl.BlockSpec(memory_space=pltpu.VMEM)],
        out_specs=[
            pl.BlockSpec((OWN_BINS, 2, 2, chans, BLOCK), lambda f: (f, 0, 0, 0, 0)),
            pl.BlockSpec(memory_space=pltpu.VMEM),
        ],
        out_shape=[
            jax.ShapeDtypeStruct((freqs, 2, 2, chans, BLOCK), jnp.float32),
            jax.ShapeDtypeStruct((freqs, 2, BLOCK, groups * depth), jnp.bfloat16),
        ],
        compiler_params=pltpu.CompilerParams(vmem_limit_bytes=16 * 2**20),
        cost_estimate=pl.CostEstimate(
            flops=2 * freqs * chans * groups * depth * 3 * BLOCK,
            bytes_accessed=freqs * 4 * chans * BLOCK * 4,
            transcendentals=0,
        ),
        name="own",
    )(place, own)


def edge_stack(first_bin, left, edge, stack, records):
    groups, bins, depth, _ = edge.shape
    return pl.pallas_call(
        functools.partial(edge_kernel, 1.0 / records, first_bin),
        in_specs=[
            pl.BlockSpec(memory_space=pltpu.VMEM),
            pl.BlockSpec(memory_space=pltpu.VMEM),
            pl.BlockSpec(memory_space=pl.ANY),
        ],
        out_specs=pl.BlockSpec(memory_space=pl.ANY),
        out_shape=jax.ShapeDtypeStruct(stack.shape, stack.dtype),
        scratch_shapes=[
            pltpu.VMEM((bins, 2, BLOCK, BLOCK), jnp.float32),
            pltpu.SemaphoreType.DMA((bins,)),
        ],
        input_output_aliases={2: 0},
        compiler_params=pltpu.CompilerParams(vmem_limit_bytes=16 * 2**20),
        cost_estimate=pl.CostEstimate(
            flops=2 * bins * BLOCK * groups * depth * 2 * BLOCK,
            bytes_accessed=bins * 2 * BLOCK * BLOCK * 4,
            transcendentals=0,
        ),
        name="edge",
    )(left, edge, stack)


def shards(record):
    chans, recs, _ = record.shape
    groups = lax.axis_size("rec")
    records = float(recs * groups)
    white = spectra(make_tables(), record.transpose(1, 2, 0))
    white = white.reshape(groups, BINS // groups, 2 * recs, chans)
    own = lax.all_to_all(white, "rec", 0, 0, tiled=True)
    freqs = own.shape[1]
    firsts = range(0, freqs, EDGE_BINS)
    edges = [turned_on(own[:, first : first + EDGE_BINS, :, chans - BLOCK :], "chan") for first in firsts]
    place = lax.axis_index("chan").reshape(1)
    stack, left = own_stack(place, own, records)
    for first, edge in zip(firsts, edges):
        stack = edge_stack(first, left, edge, stack, records)
    return stack


def solution(mesh):
    in_specs = (P("chan", "rec", None),)
    out_specs = P("rec", None, None, "chan", None)
    return jax.shard_map(shards, mesh=mesh, in_specs=in_specs, out_specs=out_specs, check_vma=False)
```
